256 devices in a mesh: group: 8 (over x, core), tensor: 32 (over y, z).
Axes of the slice: x: 4, y: 4, z: 8, core: 2. Of those that a mesh axis runs over, the one named last changes fastest.
Arguments:
- tokens: bfloat16 [8192, 8192], P(('group', 'tensor')), parts along dimension 0, may hold values from -6 to 6
- base_weight: bfloat16 [8192, 8192], P(None, 'tensor'), may hold values from -0.0625 to 0.0625
- down_pool: bfloat16 [512, 64, 8192], P(('group', 'tensor')), parts along dimension 0, may hold values from -0.0625 to 0.0625
- up_pool: bfloat16 [512, 64, 8192], P(('group', 'tensor')), parts along dimension 0, may hold values from -0.75 to 0.75
- slot_of: int32 [512], P('group'), parts along dimension 0, may hold values from 0 to 63, each once
- requested: int32 [32], P('group'), parts along dimension 0, may hold values from 0 to 63, as said below
- row_adapter: int32 [8192], P(('group', 'tensor')), parts along dimension 0, may hold values from 0 to 3
Outputs:
- projected: bfloat16 [8192, 8192], P('group', 'tensor'), parts along dimension 0
The draws below stay inside these ranges and needn't reach their ends.
There are 8 independent parts, one for each index of `group`. The reference program is written for one: setup_inputs(seed, part) draws one part's arguments, and reference() takes and returns one part's arrays. A program takes and returns all parts, laid end to end along the dimension named above; an argument that names none is the same for every part. Nothing has to cross between parts.
Inputs may be any that keep to these rules, and one draw needn't show every extreme that they name: `requested`: the 4 ids are distinct. `slot_of`: A permutation of the adapter ids.
All inputs are finite; a program needn't handle non-finite values.
Results may differ from the reference program's by a relative error of at most 0.0046.
Values may be sent and summed in bfloat16 or wider, within the bound.
No kernel may reach another device: no remote copies, remote signals or barrier semaphores. Data moves between devices by JAX's collectives and lax.ppermute only.
A program may use at most 128 MiB of HBM per device.

```python
import math
import jax
import jax.numpy as jnp
import numpy as np
from jax import lax

D = 8192
R = 64
NEW = 4
TOKENS = 1024
ADAPTERS = 64


def draw_requested(key, part):
    key = jax.random.fold_in(key, 7)
    first_key = jax.random.fold_in(key, 1)
    second_key = jax.random.fold_in(key, 2)
    others = jax.random.permutation(first_key, jnp.arange(ADAPTERS - 1, dtype=jnp.int32))[:NEW - 1]
    joined = jnp.concatenate([others, jnp.full((1,), ADAPTERS - 1, dtype=jnp.int32)])
    return jax.random.permutation(second_key, joined).astype(jnp.int32)


def place_ends(array, rng, least, largest):
    shape = array.shape
    spot = [jax.random.randint(jax.random.fold_in(rng, axis), (), 0, shape[axis]) for axis in range(len(shape))]
    array = array.at[tuple(spot)].set(least)
    longest = shape.index(max(shape))
    spot[longest] = (spot[longest] + 1) % shape[longest]
    return array.at[tuple(spot)].set(largest)


def block_scale(stream_key, extent, split, smallest, largest):
    def one(position, parts):
        steps = jax.random.uniform(jax.random.fold_in(jax.random.fold_in(stream_key, 6), position), (parts,), jnp.float32, smallest / len(split), largest / len(split))
        return jnp.repeat(jnp.exp(steps), extent[position] // parts).reshape((-1,) + (1,) * (len(extent) - position - 1))

    factor_of = one(*split[0])
    for cut in split[1:]:
        factor_of = factor_of * one(*cut)
    return factor_of


def rank_table(amount, skew):
    weights = [(1 << 20) // math.isqrt(standing ** skew) + 1 for standing in range(1, amount + 1)]
    scale = 1 + sum(weights) // (1 << 30)
    return np.cumsum(np.array([max(1, weight // scale) for weight in weights]))


def ranked_ids(key, extent, amount, lean):
    listing = rank_table(amount, lean)
    pick = jax.random.randint(jax.random.fold_in(key, 1), extent, 0, int(listing[amount - 1]))
    rank = jnp.searchsorted(jnp.asarray(listing, jnp.int32), pick, side="right")
    return jax.random.permutation(jax.random.fold_in(key, 2), amount)[rank].astype(jnp.int32)


def scatter_about(rng, dims, deviation, most, shards=(), kind=jnp.bfloat16):
    entries = jax.random.normal(rng, dims, jnp.float32) * deviation
    if len(shards) > 0:
        entries = block_scale(rng, dims, shards, -0.22, 0.18) * entries
    return jnp.clip(entries, min=-most, max=most).astype(kind)


def setup_inputs(seed: int = 0, part: int = 0) -> dict:
    key_list = jax.random.split(jax.random.key(seed), 8)
    own_keys = jax.random.split(jax.random.fold_in(key_list[7], part), 8)
    return {
        "tokens": scatter_about(own_keys[0], (TOKENS, D), 1.0, 6.0, ((0, 32),)),
        "base_weight": scatter_about(key_list[1], (D, D), D ** -0.5, 0.0625, ((1, 32),)),
        "down_pool": scatter_about(own_keys[2], (ADAPTERS, R, D), D ** -0.5, 0.0625, ((0, 32),)),
        "up_pool": scatter_about(own_keys[3], (ADAPTERS, R, D), R ** -0.5, 0.75, ((0, 32),)),
        "slot_of": jax.random.permutation(own_keys[4], ADAPTERS).astype(jnp.int32),
        "requested": draw_requested(jax.random.fold_in(jax.random.fold_in(key_list[7], part), 71), part),
        "row_adapter": place_ends(ranked_ids(own_keys[6], (TOKENS,), NEW, 2), jax.random.fold_in(own_keys[6], 3), 0, NEW - 1).astype(jnp.int32),
    }


adapter_scale = 2.0


def select_rows(products, adapter_ids, count_new, low_rank):
    onehot = (adapter_ids[:, None] == jnp.arange(count_new, dtype=jnp.int32)[None, :]).astype(jnp.float32)
    shaped = products.reshape(products.shape[0], count_new, low_rank) * onehot[:, :, None]
    return shaped.reshape(products.shape[0], count_new * low_rank).astype(jnp.bfloat16)


def reference(tokens, base_weight, down_pool, up_pool, slot_of, requested, row_adapter):
    pool_rows = slot_of[requested]
    down_cat = down_pool[pool_rows].reshape(NEW * R, D)
    up_cat = up_pool[pool_rows].reshape(NEW * R, D)
    frozen_output = jnp.dot(tokens, base_weight, preferred_element_type=jnp.float32)
    products = lax.dot_general(tokens, down_cat, (((1,), (1,)), ((), ())), preferred_element_type=jnp.float32)
    reduced_rows = select_rows(products, row_adapter, NEW, R)
    adapter_update = jnp.dot(reduced_rows, up_cat, preferred_element_type=jnp.float32)
    return (frozen_output + adapter_scale * adapter_update).astype(jnp.bfloat16)
```

```python
import jax
import jax.numpy as jnp
from jax import lax
from jax.sharding import Mesh, PartitionSpec as P

adapter_scale = 2.0


def swap(value, axis):
    return lax.all_to_all(value, axis, split_axis=0, concat_axis=0, tiled=True)


def spread(value, axis, count):
    return swap(jnp.broadcast_to(value[None], (count,) + value.shape), axis)


def after(value, *earlier):
    return lax.optimization_barrier((value,) + earlier)[0]


def per_device(nx, nc, ny, nz, tokens, base_weight, down_pool, up_pool, slot_of, requested, row_adapter):
    rows, width = tokens.shape
    width_out = base_weight.shape[1]
    held, rank, _ = down_pool.shape
    count_new = requested.shape[0]
    part = width // ny
    sub = part // (nx * nc)
    nt = ny * nz
    x, core, z = lax.axis_index("x"), lax.axis_index("core"), lax.axis_index("z")

    pool_rows = slot_of[requested]
    home, local = pool_rows // held, pool_rows % held
    home_y, home_z = home // nz, home % nz

    mine = swap(tokens.reshape(rows, ny, part).transpose(1, 0, 2), "y")
    gathered = lax.all_gather(mine.reshape(ny * rows, part), "z", axis=0, tiled=True)

    ids = spread(row_adapter, ("y", "z"), nt).reshape(ny, nz, rows)

    piece = base_weight.reshape(ny, nc * nx, sub, width_out)
    piece = lax.dynamic_index_in_dim(piece, core * nx + x, 1, keepdims=False)
    piece = swap(piece, "y").transpose(1, 0, 2).reshape(sub, ny * width_out)
    piece = spread(piece, "x", nx).reshape(nx * sub, ny * width_out)
    weight = spread(piece, "core", nc).reshape(part, ny * width_out)

    down = swap(down_pool.reshape(held, rank, ny, part).transpose(2, 0, 1, 3), "y")
    down = down.reshape(ny * held, rank, part)
    down_cat = jnp.concatenate(
        [lax.dynamic_index_in_dim(down, home_y[s] * held + local[s], 0, keepdims=False) for s in range(count_new)]
    )

    up = swap(up_pool.reshape(held, rank, ny, part).transpose(2, 0, 1, 3), "y")
    up = up.reshape(ny * held, rank, nz, width_out)
    up = jnp.stack(
        [lax.dynamic_index_in_dim(up, home_y[s] * held + local[s], 0, keepdims=False) for s in range(count_new)]
    )
    up = swap(up.transpose(2, 0, 1, 3), "z")
    up_cat = jnp.concatenate(
        [lax.dynamic_index_in_dim(up[:, s], home_z[s], 0, keepdims=False) for s in range(count_new)]
    )

    base = jnp.stack(
        [
            jnp.dot(gathered, weight[:, k * width_out : (k + 1) * width_out], preferred_element_type=jnp.float32).astype(
                jnp.bfloat16
            )
            for k in range(ny)
        ]
    )
    base = swap(base, "y")

    products = lax.dot_general(gathered, down_cat, (((1,), (1,)), ((), ())), preferred_element_type=jnp.float32)
    products = products.reshape(nz, ny, rows, count_new, rank).transpose(1, 0, 2, 3, 4)
    wanted = (ids[..., None] == jnp.arange(count_new, dtype=jnp.int32)) & (home_z == z)
    chosen = jnp.sum(jnp.where(wanted[..., None], products, 0.0), axis=3)
    chosen = swap(chosen.reshape(nt, rows, rank), ("y", "z"))
    lowered = jnp.sum(chosen, axis=0).astype(jnp.bfloat16)
    lowered = spread(lowered, ("y", "z"), nt)
    onehot = ids.reshape(nt, rows)[..., None] == jnp.arange(count_new, dtype=jnp.int32)
    lowered = jnp.where(onehot[..., None], lowered[:, :, None, :], jnp.zeros((), jnp.bfloat16))
    lowered = lowered.reshape(nt * rows, count_new * rank)
    update = jnp.dot(lowered, up_cat, preferred_element_type=jnp.float32)

    total = jnp.sum(base.astype(jnp.float32), axis=0).reshape(nz, ny, rows, width_out).transpose(1, 0, 2, 3)
    return (total.reshape(nt * rows, width_out) + adapter_scale * update).astype(jnp.bfloat16)


def solution(mesh):
    nx, nc, ny, nz = 4, 2, 4, 8
    fine = Mesh(mesh.devices.reshape(nx, nc, ny, nz), ("x", "core", "y", "z"))
    group, tensor = ("x", "core"), ("y", "z")
    both = group + tensor
    placed = (
        P(both, None),
        P(None, tensor),
        P(both, None, None),
        P(both, None, None),
        P(group),
        P(group),
        P(both),
    )

    def step(*args):
        return per_device(nx, nc, ny, nz, *args)

    return jax.shard_map(step, mesh=fine, in_specs=placed, out_specs=P(group, tensor), check_vma=False)
```

```python
import functools

import jax
import jax.numpy as jnp
from jax import lax
from jax.experimental import pallas as pl
from jax.experimental.pallas import tpu as pltpu
from jax.sharding import Mesh, PartitionSpec as P

adapter_scale = 2.0
vmem_bytes = 48 * 1024 * 1024


def swap(value, axis):
    return lax.all_to_all(value, axis, split_axis=0, concat_axis=0, tiled=True)


def spread(value, axis, count):
    return swap(jnp.broadcast_to(value[None], (count,) + value.shape), axis)


def after(value, *earlier):
    return lax.optimization_barrier((value,) + earlier)[0]


def shift(value, axis, size, by):
    return lax.ppermute(value, axis, [(i, (i + by) % size) for i in range(size)])


def doubled(value, axis, size, place):
    bit = 1
    while bit < size:
        other = lax.ppermute(value, axis, [(i, i ^ bit) for i in range(size)])
        high = (place & bit) != 0
        value = jnp.concatenate([jnp.where(high, other, value), jnp.where(high, value, other)])
        bit *= 2
    return value


def base_kernel(core_ref, rows_ref, mine_ref, other_ref, out_ref):
    half = mine_ref.shape[0]
    rows = rows_ref.shape[0] * rows_ref.shape[2]
    core = core_ref[0]
    first = rows_ref[:, 0, :, pl.ds(pl.multiple_of(core * half, half), half)].reshape(rows, half)
    second = rows_ref[:, 0, :, pl.ds(pl.multiple_of((1 - core) * half, half), half)].reshape(rows, half)
    total = jnp.dot(first, mine_ref[...], preferred_element_type=jnp.float32)
    total += jnp.dot(second, other_ref[...], preferred_element_type=jnp.float32)
    width = out_ref.shape[2]
    for k in range(out_ref.shape[0]):
        out_ref[k] = total[:, k * width : (k + 1) * width].astype(out_ref.dtype)


def base_parts(core, gathered, mine, other, ny, nz, rows, width_out):
    part = gathered.shape[1]
    whole = pl.BlockSpec(mine.shape, lambda i, c: (0, 0))
    return pl.pallas_call(
        base_kernel,
        out_shape=jax.ShapeDtypeStruct((ny, ny * nz * rows, width_out), jnp.bfloat16),
        grid_spec=pltpu.PrefetchScalarGridSpec(
            num_scalar_prefetch=1,
            grid=(ny,),
            in_specs=[pl.BlockSpec((nz, 1, rows, part), lambda i, c: (0, i, 0, 0)), whole, whole],
            out_specs=pl.BlockSpec((ny, nz * rows, width_out), lambda i, c: (0, i, 0)),
        ),
        compiler_params=pltpu.CompilerParams(vmem_limit_bytes=vmem_bytes),
        cost_estimate=pl.CostEstimate(
            flops=2 * ny * nz * rows * part * ny * width_out, bytes_accessed=10 * 1024 * 1024, transcendentals=0
        ),
        name="base_parts",
    )(core, gathered.reshape(nz, ny, rows, part), mine, other)


def chosen_kernel(count, wanted_ref, slot_ref, rows_ref, ids_ref, *rest):
    downs, out_ref = rest[:count], rest[count]
    nz, _, rows, part = rows_ref.shape
    rank = downs[0].shape[1]
    lines = rows_ref[:, 0].reshape(nz * rows, part)
    lane = lax.broadcasted_iota(jnp.int32, (nz * rows, 2 * rank), 1)
    total = jnp.zeros((nz * rows, 2 * rank), jnp.float32)
    for s in range(0, count, 2):
        both = jnp.concatenate([downs[s][0], downs[s + 1][0]], axis=0)
        product = lax.dot_general(lines, both, (((1,), (1,)), ((), ())), preferred_element_type=jnp.float32)
        target = jnp.where(lane < rank, wanted_ref[s], wanted_ref[s + 1])
        total += jnp.where(ids_ref[...] == target, product, 0.0)
    total = total[:, :rank] + total[:, rank:]
    for k in range(nz):
        piece = total[k * rows : (k + 1) * rows]
        out_ref[k] = jnp.concatenate([piece[: rows // 2], piece[rows // 2 :]], axis=1)


def chosen_parts(wanted, slots, gathered, ids, down, count, ny, nz, rows):
    part = gathered.shape[1]
    _, rank, _ = down.shape

    def slot_spec(s):
        return pl.BlockSpec((1, rank, part), lambda i, w, p: (p[s], 0, 0))

    return pl.pallas_call(
        functools.partial(chosen_kernel, count),
        out_shape=jax.ShapeDtypeStruct((ny * nz, rows // 2, 2 * rank), jnp.float32),
        grid_spec=pltpu.PrefetchScalarGridSpec(
            num_scalar_prefetch=2,
            grid=(ny,),
            in_specs=[
                pl.BlockSpec((nz, 1, rows, part), lambda i, w, p: (0, i, 0, 0)),
                pl.BlockSpec((nz * rows, 2 * rank), lambda i, w, p: (i, 0)),
            ]
            + [slot_spec(s) for s in range(count)],
            out_specs=pl.BlockSpec((nz, rows // 2, 2 * rank), lambda i, w, p: (i, 0, 0)),
        ),
        compiler_params=pltpu.CompilerParams(vmem_limit_bytes=vmem_bytes),
        cost_estimate=pl.CostEstimate(
            flops=2 * ny * nz * rows * part * count * rank, bytes_accessed=6 * 1024 * 1024, transcendentals=0
        ),
        name="chosen_parts",
    )(wanted, slots, gathered.reshape(nz, ny, rows, part), ids, *([down] * count))


def final_kernel(count, base_ref, low_ref, ids_ref, up_ref, out_ref):
    nz, half, both = low_ref.shape
    rank = both // 2
    low = jnp.concatenate(
        [low_ref[k][:, h * rank : (h + 1) * rank] for k in range(nz) for h in range(2)], axis=0
    ).astype(jnp.float32)
    low = jnp.concatenate([low, low], axis=1)
    lane = lax.broadcasted_iota(jnp.int32, low.shape, 1)
    update = jnp.zeros(out_ref.shape, jnp.float32)
    for s in range(0, count, 2):
        target = jnp.where(lane < rank, s, s + 1)
        kept = jnp.where(ids_ref[...] == target, low, 0.0).astype(jnp.bfloat16)
        update += jnp.dot(kept, up_ref[s * rank : (s + 2) * rank], preferred_element_type=jnp.float32)
    out_ref[...] = (base_ref[...].astype(jnp.float32) + adapter_scale * update).astype(out_ref.dtype)


def final_rows(base, low, ids, up_cat, count, ny, nz):
    tall, width_out = base.shape
    block = tall // ny
    return pl.pallas_call(
        functools.partial(final_kernel, count),
        out_shape=jax.ShapeDtypeStruct((tall, width_out), jnp.bfloat16),
        grid=(ny,),
        in_specs=[
            pl.BlockSpec((block, width_out), lambda i: (i, 0)),
            pl.BlockSpec((nz,) + low.shape[1:], lambda i: (i, 0, 0)),
            pl.BlockSpec((block, ids.shape[1]), lambda i: (i, 0)),
            pl.BlockSpec(up_cat.shape, lambda i: (0, 0)),
        ],
        out_specs=pl.BlockSpec((block, width_out), lambda i: (i, 0)),
        compiler_params=pltpu.CompilerParams(vmem_limit_bytes=vmem_bytes),
        cost_estimate=pl.CostEstimate(
            flops=2 * tall * up_cat.shape[0] * width_out, bytes_accessed=2 * 1024 * 1024, transcendentals=0
        ),
        name="final_rows",
    )(base, low, ids, up_cat)


def per_device(nx, nc, ny, nz, tokens, base_weight, down_pool, up_pool, slot_of, requested, row_adapter):
    rows, width = tokens.shape
    width_out = base_weight.shape[1]
    held, rank, _ = down_pool.shape
    count_new = requested.shape[0]
    part = width // ny
    sub = part // (nx * nc)
    nt = ny * nz
    x, core, y, z = [lax.axis_index(a) for a in ("x", "core", "y", "z")]

    blocks = jnp.stack([tokens[:, k * part : (k + 1) * part] for k in range(ny)])
    mine = swap(blocks, "y")
    gathered = lax.all_gather(mine.reshape(ny * rows, part), "z", axis=0, tiled=True)

    pool_rows = slot_of[requested]
    home, local = pool_rows // held, pool_rows % held
    home_y, home_z = home // nz, home % nz

    ids = doubled(row_adapter.reshape(1, rows), "z", nz, z)
    ids = doubled(ids, "y", ny, y)
    ids = jnp.broadcast_to(ids.reshape(nt * rows, 1), (nt * rows, 2 * rank))

    piece = base_weight.reshape(ny, nc * nx, sub, width_out)
    piece = lax.dynamic_index_in_dim(piece, core * nx + x, 1, keepdims=False)
    piece = swap(after(piece, mine), "y").transpose(1, 0, 2).reshape(sub, ny * width_out)
    piece = spread(piece, "x", nx).reshape(nx * sub, ny * width_out)
    other = shift(piece, "core", nc, 1)

    down = jnp.stack([down_pool[:, :, k * part : (k + 1) * part] for k in range(ny)])
    down = swap(after(down, piece), "y").reshape(ny * held, rank, part)

    ups = []
    for d in range(ny):
        block = lax.dynamic_slice_in_dim(up_pool, ((y + d) % ny) * part, part, 2)
        ups.append(shift(after(block, mine), "y", ny, d) if d else block)
    ups = jnp.stack(ups)
    ups = jnp.stack([ups[(y - home_y[s]) % ny, local[s]] for s in range(count_new)])
    cols = []
    for d in range(nz):
        block = lax.dynamic_slice_in_dim(ups, ((z + d) % nz) * width_out, width_out, 2)
        cols.append(shift(block, "z", nz, d) if d else block)
    cols = jnp.stack(cols)
    up_cat = jnp.concatenate([cols[(z - home_z[s]) % nz, s] for s in range(count_new)])

    base = base_parts(core.astype(jnp.int32).reshape(1), gathered, piece, other, ny, nz, rows, width_out)
    base = lax.psum_scatter(base, "y", scatter_dimension=0, tiled=True)[0]

    wanted = jnp.where(home_z == z, jnp.arange(count_new, dtype=jnp.int32), -1)
    slots = home_y * held + local
    chosen = swap(chosen_parts(wanted, slots, gathered, ids, down, count_new, ny, nz, rows), ("y", "z"))
    lowered = jnp.sum(chosen, axis=0).astype(jnp.bfloat16)
    lowered = spread(lowered, ("y", "z"), nt)
    return final_rows(base, lowered, ids, up_cat, count_new, ny, nz)


def solution(mesh):
    nx, nc, ny, nz = 4, 2, 4, 8
    fine = Mesh(mesh.devices.reshape(nx, nc, ny, nz), ("x", "core", "y", "z"))
    group, tensor = ("x", "core"), ("y", "z")
    both = group + tensor
    placed = (
        P(both, None),
        P(None, tensor),
        P(both, None, None),
        P(both, None, None),
        P(group),
        P(group),
        P(both),
    )

    def step(*args):
        return per_device(nx, nc, ny, nz, *args)

    return jax.shard_map(step, mesh=fine, in_specs=placed, out_specs=P(group, tensor), check_vma=False)
```

```python
import functools

import jax
import jax.numpy as jnp
from jax import lax
from jax.experimental import pallas as pl
from jax.experimental.pallas import tpu as pltpu
from jax.sharding import Mesh, PartitionSpec as P

adapter_scale = 2.0
mebibyte = 1024 * 1024


def swap(value, axis):
    return lax.all_to_all(value, axis, split_axis=0, concat_axis=0, tiled=True)


def after(value, *earlier):
    return lax.optimization_barrier((value,) + earlier)[0]


def shift(value, axis, size, by):
    return lax.ppermute(value, axis, [(i, (i + by) % size) for i in range(size)])


def doubled(value, axis, size, place):
    bit = 1
    while bit < size:
        other = lax.ppermute(value, axis, [(i, i ^ bit) for i in range(size)])
        high = (place & bit) != 0
        value = jnp.concatenate([jnp.where(high, other, value), jnp.where(high, value, other)])
        bit *= 2
    return value


def send_kernel(place_ref, tokens_ref, *rest):
    half = len(rest) // 2
    rows = tokens_ref.shape[0]
    for d in range(half):
        block_ref, out_ref = rest[d], rest[half + d]
        part, width = out_ref.shape[1], block_ref.shape[2]
        short = out_ref.shape[0] - rows
        first = (place_ref[2] + d) % half * part
        out_ref[:rows] = tokens_ref[:, pl.ds(pl.multiple_of(first, part), part)]
        for k in range(part // width):
            out_ref[rows:, k * width : (k + 1) * width] = block_ref[0, k * short : (k + 1) * short]


def send_parts(place, tokens, weights, ny, group):
    rows, width = tokens.shape
    _, sub, width_out = weights.shape
    part = width // ny
    short = sub * width_out // part

    def block_spec(d):
        return pl.BlockSpec(
            (1, sub, width_out), lambda i, p: ((p[2] + d) % ny * group + p[1] * (group // 2) + p[0], 0, 0)
        )

    return pl.pallas_call(
        send_kernel,
        out_shape=[jax.ShapeDtypeStruct((rows + short, part), tokens.dtype)] * ny,
        grid_spec=pltpu.PrefetchScalarGridSpec(
            num_scalar_prefetch=1,
            grid=(1,),
            in_specs=[pl.BlockSpec(tokens.shape, lambda i, p: (0, 0))] + [block_spec(d) for d in range(ny)],
            out_specs=[pl.BlockSpec((rows + short, part), lambda i, p: (0, 0))] * ny,
        ),
        compiler_params=pltpu.CompilerParams(vmem_limit_bytes=60 * mebibyte),
        cost_estimate=pl.CostEstimate(flops=0, bytes_accessed=2 * mebibyte, transcendentals=0),
        name="send_parts",
    )(place, tokens, *([weights] * ny))


def arrive_kernel(*refs):
    arrived, far_ref, piece_ref = refs[:-2], refs[-2], refs[-1]
    rows = far_ref.shape[0] // len(arrived)
    width = piece_ref.shape[1] // len(arrived)
    short = arrived[0].shape[0] - rows
    for d, ref in enumerate(arrived):
        far_ref[d * rows : (d + 1) * rows] = ref[:rows]
        for k in range(ref.shape[1] // width):
            piece_ref[k * short : (k + 1) * short, d * width : (d + 1) * width] = ref[
                rows:, k * width : (k + 1) * width
            ]


def arrive_parts(arrived, rows, sub, width_out):
    count = len(arrived)
    part = arrived[0].shape[1]
    return pl.pallas_call(
        arrive_kernel,
        out_shape=[
            jax.ShapeDtypeStruct((count * rows, part), arrived[0].dtype),
            jax.ShapeDtypeStruct((sub, count * width_out), arrived[0].dtype),
        ],
        compiler_params=pltpu.CompilerParams(vmem_limit_bytes=8 * mebibyte),
        cost_estimate=pl.CostEstimate(flops=0, bytes_accessed=2 * mebibyte, transcendentals=0),
        name="arrive_parts",
    )(*arrived)


def cut_kernel(*refs):
    count = (len(refs) - 2) // 3
    pools, outs, held, arrived, left = refs[:count], refs[count : 2 * count], refs[2 * count : -2], refs[-2], refs[-1]

    def pool_of(j):
        return pltpu.make_async_copy(pools[j], held[j], arrived.at[j])

    def piece_of(j, k):
        part = outs[j].shape[3]
        return pltpu.make_async_copy(held[j].at[:, :, pl.ds(k * part, part)], outs[j].at[k], left.at[j, k])

    for j in range(count):
        pool_of(j).start()
    for j in range(count):
        pool_of(j).wait()
        for k in range(outs[j].shape[0]):
            piece_of(j, k).start()
    for j in range(count):
        for k in range(outs[j].shape[0]):
            piece_of(j, k).wait()


def cut_parts(pools, count):
    held, rank, width = pools[0].shape
    where = pl.BlockSpec(memory_space=pl.ANY)
    return pl.pallas_call(
        cut_kernel,
        out_shape=[jax.ShapeDtypeStruct((count, held, rank, width // count), p.dtype) for p in pools],
        in_specs=[where] * len(pools),
        out_specs=[where] * len(pools),
        scratch_shapes=[pltpu.VMEM(p.shape, p.dtype) for p in pools]
        + [pltpu.SemaphoreType.DMA((len(pools),)), pltpu.SemaphoreType.DMA((len(pools), count))],
        compiler_params=pltpu.CompilerParams(vmem_limit_bytes=60 * mebibyte),
        cost_estimate=pl.CostEstimate(flops=0, bytes_accessed=8 * mebibyte, transcendentals=0),
        name="cut_parts",
    )(*pools)


def pick_kernel(slot_ref, wanted_ref, pool_ref, out_ref):
    width = out_ref.shape[3]
    wanted = wanted_ref[pl.program_id(0)] != 0
    for k in range(out_ref.shape[0]):
        piece = pool_ref[0, :, k * width : (k + 1) * width]
        out_ref[k, 0] = jnp.where(wanted, piece, jnp.zeros_like(piece))


def pick_parts(slots, wanted, pool, pieces):
    _, rank, part = pool.shape
    count = slots.shape[0]
    width = part // pieces
    return pl.pallas_call(
        pick_kernel,
        out_shape=jax.ShapeDtypeStruct((pieces, count, rank, width), pool.dtype),
        grid_spec=pltpu.PrefetchScalarGridSpec(
            num_scalar_prefetch=2,
            grid=(count,),
            in_specs=[pl.BlockSpec((1, rank, part), lambda i, s, w: (s[i], 0, 0))],
            out_specs=pl.BlockSpec((pieces, 1, rank, width), lambda i, s, w: (0, i, 0, 0)),
        ),
        compiler_params=pltpu.CompilerParams(vmem_limit_bytes=12 * mebibyte),
        cost_estimate=pl.CostEstimate(flops=0, bytes_accessed=4 * count * rank * part, transcendentals=0),
        name="pick_parts",
    )(slots, wanted, pool)


def order_kernel(place_ref, *refs):
    out_ref = refs[-1]
    count = len(refs) - 1
    sub = refs[0].shape[0]
    for e in range(count):
        first = (place_ref[0] + count - e) % count * sub
        out_ref[pl.ds(pl.multiple_of(first, sub), sub)] = refs[e][...]


def order_parts(place, pieces):
    sub, wide = pieces[0].shape
    near = pl.BlockSpec(memory_space=pltpu.VMEM)
    return pl.pallas_call(
        order_kernel,
        out_shape=jax.ShapeDtypeStruct((len(pieces) * sub, wide), pieces[0].dtype),
        in_specs=[pl.BlockSpec(memory_space=pltpu.SMEM)] + [near] * len(pieces),
        out_specs=near,
        compiler_params=pltpu.CompilerParams(vmem_limit_bytes=8 * mebibyte),
        cost_estimate=pl.CostEstimate(flops=0, bytes_accessed=4 * mebibyte, transcendentals=0),
        name="order_parts",
    )(place, *pieces)


def part_kernel(place_ref, wanted_ref, slot_ref, gathered_ref, mine_ref, other_ref, pool_ref, ids_ref, *rest):
    ny = gathered_ref.shape[1]
    outs, chosen_ref = rest[:ny], rest[ny]
    rows_ref, weight_ref, down_ref, held_ref, arrived, weighed, downed, left = rest[ny + 1 :]
    half = mine_ref.shape[0]
    _, nz, rows, part = rows_ref.shape
    width = outs[0].shape[1]
    rank = pool_ref.shape[1]
    count = slot_ref.shape[0]
    block = nz * rows
    blocks = 2

    def owner_of(k):
        return (place_ref[2] + ny - k) % ny

    def owned(k):
        return pl.ds(pl.multiple_of(owner_of(k) * block, block), block)

    def lines_of(k):
        return pltpu.make_async_copy(gathered_ref.at[:, k], rows_ref.at[k], arrived.at[k])

    def weight_of(j, ref):
        return pltpu.make_async_copy(ref, weight_ref.at[j], weighed.at[j])

    def down_of(s):
        return pltpu.make_async_copy(pool_ref.at[slot_ref[s]], down_ref.at[pl.ds(s * rank, rank)], downed.at[s])

    def result_of(d, k):
        return pltpu.make_async_copy(held_ref.at[d, k], outs[d].at[owned(k)], left.at[d, k])

    weight_of(0, mine_ref).start()
    for k in range(blocks):
        lines_of(k).start()
    weight_of(1, other_ref).start()
    for k in range(blocks, ny):
        lines_of(k).start()
    for s in range(count):
        down_of(s).start()

    for step in range(ny // blocks):
        for k in range(blocks):
            lines_of(step * blocks + k).wait()
        here = pl.ds(step * blocks, blocks)
        total = None
        for j, (ref, core) in enumerate(((mine_ref, place_ref[1]), (other_ref, 1 - place_ref[1]))):
            if step == 0:
                weight_of(j, ref).wait()
            lines = rows_ref[here, :, :, pl.ds(pl.multiple_of(core * half, half), half)].reshape(blocks * block, half)
            product = jnp.dot(lines, weight_ref[j], preferred_element_type=jnp.float32)
            total = product if total is None else total + product
        for k in range(blocks):
            for d in range(ny):
                piece = total[k * block : (k + 1) * block, d * width : (d + 1) * width]
                held_ref[d, step * blocks + k] = piece.astype(held_ref.dtype)
                result_of(d, step * blocks + k).start()

    for s in range(count):
        down_of(s).wait()
    lane = lax.broadcasted_iota(jnp.int32, (block, 2 * rank), 1)
    targets = [jnp.where(lane < rank, wanted_ref[s], wanted_ref[s + 1]) for s in range(0, count, 2)]
    for k in range(ny):
        product = lax.dot_general(
            rows_ref[k].reshape(block, part),
            down_ref[...],
            (((1,), (1,)), ((), ())),
            preferred_element_type=jnp.float32,
        )
        ids = ids_ref[owned(k)]
        chosen = jnp.zeros((block, 2 * rank), jnp.float32)
        for j, target in enumerate(targets):
            chosen += jnp.where(ids == target, product[:, 2 * j * rank : 2 * (j + 1) * rank], 0.0)
        chosen = chosen[:, :rank] + chosen[:, rank:]
        for j in range(nz):
            piece = chosen[j * rows : (j + 1) * rows]
            chosen_ref[owner_of(k) * nz + j] = jnp.concatenate([piece[: rows // 2], piece[rows // 2 :]], axis=1)
    for k in range(ny):
        for d in range(ny):
            result_of(d, k).wait()


def part_products(place, wanted, slots, gathered, mine, other, down, ids, width_out):
    nz, ny, rows, part = gathered.shape
    _, rank, _ = down.shape
    count = slots.shape[0]
    scalars = pl.BlockSpec(memory_space=pltpu.SMEM)
    where = pl.BlockSpec(memory_space=pl.ANY)
    near = pl.BlockSpec(memory_space=pltpu.VMEM)
    kind = gathered.dtype
    *base, chosen = pl.pallas_call(
        part_kernel,
        out_shape=[jax.ShapeDtypeStruct((ny * nz * rows, width_out), kind)] * ny
        + [jax.ShapeDtypeStruct((ny * nz, rows // 2, 2 * rank), jnp.float32)],
        in_specs=[scalars, scalars, scalars, where, where, where, where, near],
        out_specs=[where] * ny + [near],
        scratch_shapes=[
            pltpu.VMEM((ny, nz, rows, part), kind),
            pltpu.VMEM((2,) + mine.shape, kind),
            pltpu.VMEM((count * rank, part), kind),
            pltpu.VMEM((ny, ny, nz * rows, width_out), kind),
            pltpu.SemaphoreType.DMA((ny,)),
            pltpu.SemaphoreType.DMA((2,)),
            pltpu.SemaphoreType.DMA((count,)),
            pltpu.SemaphoreType.DMA((ny, ny)),
        ],
        compiler_params=pltpu.CompilerParams(vmem_limit_bytes=50 * mebibyte),
        cost_estimate=pl.CostEstimate(
            flops=2 * ny * nz * rows * part * (ny * width_out + count * rank),
            bytes_accessed=12 * mebibyte,
            transcendentals=0,
        ),
        name="part_products",
    )(place, wanted, slots, gathered, mine, other, down, ids)
    return base, chosen


def lower_kernel(parts_ref, out_ref):
    low = jnp.sum(parts_ref[...], axis=0).astype(out_ref.dtype)
    for k in range(out_ref.shape[0]):
        out_ref[k] = low


def lower_parts(parts):
    near = pl.BlockSpec(memory_space=pltpu.VMEM)
    return pl.pallas_call(
        lower_kernel,
        out_shape=jax.ShapeDtypeStruct(parts.shape, jnp.bfloat16),
        in_specs=[near],
        out_specs=near,
        compiler_params=pltpu.CompilerParams(vmem_limit_bytes=8 * mebibyte),
        cost_estimate=pl.CostEstimate(flops=0, bytes_accessed=mebibyte, transcendentals=0),
        name="lower_parts",
    )(parts)


def final_kernel(low_ref, ids_ref, up_ref, *rest):
    base, out_ref = rest[:-1], rest[-1]
    count, rank, width = up_ref.shape
    low = jnp.concatenate(
        [low_ref[k][:, h * rank : (h + 1) * rank] for k in range(low_ref.shape[0]) for h in range(2)], axis=0
    )
    low = jnp.concatenate([low, low], axis=1).astype(jnp.float32)
    lane = lax.broadcasted_iota(jnp.int32, low.shape, 1)
    kept = [
        jnp.where(ids_ref[...] == jnp.where(lane < rank, s, s + 1), low, 0.0).astype(jnp.bfloat16)
        for s in range(0, count, 2)
    ]
    up = up_ref[...].reshape(count * rank, width)
    update = jnp.dot(jnp.concatenate(kept, axis=1), up, preferred_element_type=jnp.float32)
    total = base[0][...].astype(jnp.float32)
    for ref in base[1:]:
        total += ref[...].astype(jnp.float32)
    out_ref[...] = (total + adapter_scale * update).astype(out_ref.dtype)


def final_rows(low, ids, ups, base):
    tall, width_out = base[0].shape
    count, rank, _ = ups.shape
    near = pl.BlockSpec(memory_space=pltpu.VMEM)
    return pl.pallas_call(
        final_kernel,
        out_shape=jax.ShapeDtypeStruct((tall, width_out), jnp.bfloat16),
        in_specs=[near] * (3 + len(base)),
        out_specs=near,
        compiler_params=pltpu.CompilerParams(vmem_limit_bytes=16 * mebibyte),
        cost_estimate=pl.CostEstimate(
            flops=2 * tall * count * rank * width_out, bytes_accessed=4 * mebibyte, transcendentals=0
        ),
        name="final_rows",
    )(low, ids, ups, *base)


def per_device(nx, nc, ny, nz, tokens, base_weight, down_pool, up_pool, slot_of, requested, row_adapter):
    rows, width = tokens.shape
    width_out = base_weight.shape[1]
    held, rank, _ = down_pool.shape
    count_new = requested.shape[0]
    part = width // ny
    sub = part // (nx * nc)
    nt = ny * nz
    x, core, y, z = [lax.axis_index(a).astype(jnp.int32) for a in ("x", "core", "y", "z")]
    place = jnp.stack([x, core, y, z])

    weights = base_weight.reshape(ny * nc * nx, sub, width_out)
    sent = send_parts(place, tokens, weights, ny, nc * nx)
    down, up = cut_parts([down_pool, after(up_pool, sent[1])], ny)
    arrived = [after(sent[0], down, up)] + [shift(sent[d], "y", ny, d) for d in range(1, ny)]
    far, piece = arrive_parts(arrived, rows, sub, width_out)
    gathered = lax.all_gather(far, "z", axis=0, tiled=True).reshape(nz, ny, rows, part)

    pool_rows = slot_of[requested]
    home, local = pool_rows // held, pool_rows % held
    home_y, home_z = home // nz, home % nz
    slots = home_y * held + local

    down = swap(down, "y").reshape(ny * held, rank, part)

    ids = doubled(after(row_adapter, sent[1]).reshape(1, rows), "z", nz, z)
    ids = doubled(ids, "y", ny, y)

    piece = order_parts(place, [shift(piece, "x", nx, e) if e else piece for e in range(nx)])
    other = shift(piece, "core", nc, 1)

    ups = swap(after(up, down, ids), "y").reshape(ny * held, rank, part)
    ups = pick_parts(slots, (home_z == z).astype(jnp.int32), ups, nz)
    other = after(other, ups)
    ups = lax.psum_scatter(ups, "z", scatter_dimension=0, tiled=True)[0]

    wanted = jnp.where(home_z == z, jnp.arange(count_new, dtype=jnp.int32), -1)
    ids = jnp.broadcast_to(ids.reshape(nt * rows, 1), (nt * rows, 2 * rank))
    base, chosen = part_products(place, wanted, slots, gathered, piece, other, down, ids, width_out)
    base = [shift(part, "y", ny, ny - d) if d else part for d, part in enumerate(base)]
    lowered = swap(lower_parts(swap(chosen, ("y", "z"))), ("y", "z"))
    return final_rows(lowered, ids, ups, base)


def solution(mesh):
    nx, nc, ny, nz = 4, 2, 4, 8
    fine = Mesh(mesh.devices.reshape(nx, nc, ny, nz), ("x", "core", "y", "z"))
    group, tensor = ("x", "core"), ("y", "z")
    both = group + tensor
    placed = (
        P(both, None),
        P(None, tensor),
        P(both, None, None),
        P(both, None, None),
        P(group),
        P(group),
        P(both),
    )

    def step(*args):
        return per_device(nx, nc, ny, nz, *args)

    return jax.shard_map(step, mesh=fine, in_specs=placed, out_specs=P(group, tensor), check_vma=False)
```

```python
import functools

import jax
import jax.numpy as jnp
from jax import lax
from jax.experimental import pallas as pl
from jax.experimental.pallas import tpu as pltpu
from jax.sharding import Mesh, PartitionSpec as P

adapter_scale = 2.0
mebibyte = 1024 * 1024


def swap(value, axis):
    return lax.all_to_all(value, axis, split_axis=0, concat_axis=0, tiled=True)


def after(value, *earlier):
    return lax.optimization_barrier((value,) + earlier)[0]


def shift(value, axis, size, by):
    return lax.ppermute(value, axis, [(i, (i + by) % size) for i in range(size)])


def send_kernel(place_ref, tokens_ref, *outs):
    part = outs[0].shape[1]
    for d, out_ref in enumerate(outs):
        first = (place_ref[2] + d) % len(outs) * part
        out_ref[...] = tokens_ref[:, pl.ds(pl.multiple_of(first, part), part)]


def send_parts(place, tokens, count):
    rows, width = tokens.shape
    near = pl.BlockSpec(memory_space=pltpu.VMEM)
    return pl.pallas_call(
        send_kernel,
        out_shape=[jax.ShapeDtypeStruct((rows, width // count), tokens.dtype)] * count,
        in_specs=[pl.BlockSpec(memory_space=pltpu.SMEM), near],
        out_specs=[near] * count,
        compiler_params=pltpu.CompilerParams(vmem_limit_bytes=8 * mebibyte),
        cost_estimate=pl.CostEstimate(flops=0, bytes_accessed=mebibyte, transcendentals=0),
        name="send_parts",
    )(place, tokens)


def cut_kernel(*refs):
    count = len(refs) // 2 - 1
    pools, out, held, arrived, left = refs[:count], refs[count], refs[count + 1 : -2], refs[-2], refs[-1]
    slots = pools[0].shape[0]
    part = out.shape[3]

    def pool_of(j):
        return pltpu.make_async_copy(pools[j], held[j], arrived.at[j])

    def piece_of(j, k):
        source = held[j].at[:, :, pl.ds(k * part, part)]
        return pltpu.make_async_copy(source, out.at[k, pl.ds(j * slots, slots)], left.at[j, k])

    for j in range(count):
        pool_of(j).start()
    for j in range(count):
        pool_of(j).wait()
        for k in range(out.shape[0]):
            piece_of(j, k).start()
    for j in range(count):
        for k in range(out.shape[0]):
            piece_of(j, k).wait()


def cut_parts(pools, count):
    held, rank, width = pools[0].shape
    where = pl.BlockSpec(memory_space=pl.ANY)
    return pl.pallas_call(
        cut_kernel,
        out_shape=jax.ShapeDtypeStruct((count, len(pools) * held, rank, width // count), pools[0].dtype),
        in_specs=[where] * len(pools),
        out_specs=where,
        scratch_shapes=[pltpu.VMEM(p.shape, p.dtype) for p in pools]
        + [pltpu.SemaphoreType.DMA((len(pools),)), pltpu.SemaphoreType.DMA((len(pools), count))],
        compiler_params=pltpu.CompilerParams(vmem_limit_bytes=60 * mebibyte),
        cost_estimate=pl.CostEstimate(flops=0, bytes_accessed=8 * mebibyte, transcendentals=0),
        name="cut_parts",
    )(*pools)


def order_kernel(place_ref, *refs):
    out_ref = refs[-1]
    count = len(refs) - 1
    sub = refs[0].shape[0]
    for e in range(count):
        first = (place_ref[0] + count - e) % count * sub
        out_ref[pl.ds(pl.multiple_of(first, sub), sub)] = refs[e][...]


def order_parts(place, pieces):
    sub, wide = pieces[0].shape
    near = pl.BlockSpec(memory_space=pltpu.VMEM)
    return pl.pallas_call(
        order_kernel,
        out_shape=jax.ShapeDtypeStruct((len(pieces) * sub, wide), pieces[0].dtype),
        in_specs=[pl.BlockSpec(memory_space=pltpu.SMEM)] + [near] * len(pieces),
        out_specs=near,
        compiler_params=pltpu.CompilerParams(vmem_limit_bytes=8 * mebibyte),
        cost_estimate=pl.CostEstimate(flops=0, bytes_accessed=4 * mebibyte, transcendentals=0),
        name="order_parts",
    )(place, *pieces)


def local_kernel(
    place_ref, wanted_ref, slot_ref, rows_ref, pool_ref, out_ref, ups_ref, down_ref, up_ref, downed, upped
):
    nz, ny, rows, part = rows_ref.shape
    rank = pool_ref.shape[1]
    count = slot_ref.shape[0] // 2
    width = ups_ref.shape[3]
    steps = 2
    share = nz // steps

    def up_of(s):
        return pltpu.make_async_copy(pool_ref.at[slot_ref[s]], up_ref.at[s], upped.at[s])

    def down_of(s):
        lines = pl.ds(s * rank, rank)
        return pltpu.make_async_copy(pool_ref.at[slot_ref[count + s]], down_ref.at[lines], downed.at[s])

    for s in range(count):
        down_of(s).start()
    for s in range(count):
        up_of(s).start()
    for s in range(count):
        down_of(s).wait()

    lane = lax.broadcasted_iota(jnp.int32, (rows, count * rank), 1) // rank
    wanted = lane < 0
    for s in range(count):
        wanted = wanted | ((lane == s) & (wanted_ref[s] != 0))
    for i in range(steps):
        product = lax.dot_general(
            rows_ref[i * share : (i + 1) * share].reshape(share * ny * rows, part),
            down_ref[...],
            (((1,), (1,)), ((), ())),
            preferred_element_type=jnp.float32,
        )
        for j in range(share):
            for k in range(ny):
                first = (j * ny + k) * rows
                piece = jnp.where(wanted, product[first : first + rows], 0.0)
                out_ref[(place_ref[2] + ny - k) % ny * nz + i * share + j] = piece.astype(out_ref.dtype)
    for s in range(count):
        up_of(s).wait()
        for k in range(nz):
            piece = up_ref[s, :, k * width : (k + 1) * width]
            ups_ref[k, s] = jnp.where(wanted_ref[s] != 0, piece, jnp.zeros_like(piece))


def local_parts(place, wanted, slots, gathered, pools, width_out):
    nz, ny, rows, part = gathered.shape
    _, rank, _ = pools.shape
    count = wanted.shape[0]
    kind = gathered.dtype
    scalars = pl.BlockSpec(memory_space=pltpu.SMEM)
    where = pl.BlockSpec(memory_space=pl.ANY)
    near = pl.BlockSpec(memory_space=pltpu.VMEM)
    return pl.pallas_call(
        local_kernel,
        out_shape=[
            jax.ShapeDtypeStruct((ny * nz, rows, count * rank), kind),
            jax.ShapeDtypeStruct((nz, count, rank, width_out), kind),
        ],
        in_specs=[scalars, scalars, scalars, near, where],
        out_specs=[near, near],
        scratch_shapes=[
            pltpu.VMEM((count * rank, part), kind),
            pltpu.VMEM((count, rank, part), kind),
            pltpu.SemaphoreType.DMA((count,)),
            pltpu.SemaphoreType.DMA((count,)),
        ],
        compiler_params=pltpu.CompilerParams(vmem_limit_bytes=14 * mebibyte),
        cost_estimate=pl.CostEstimate(
            flops=2 * ny * nz * rows * part * count * rank, bytes_accessed=8 * mebibyte, transcendentals=0
        ),
        name="local_parts",
    )(place, wanted, slots, gathered, pools)


def base_kernel(place_ref, rows_ref, mine_ref, other_ref, *outs):
    nz, ny, rows, part = rows_ref.shape
    half = mine_ref.shape[0]
    width = outs[0].shape[1]
    steps = 2
    tall = nz // steps * ny * rows
    for step in range(steps):
        here = pl.ds(step * (nz // steps), nz // steps)
        total = None
        for ref, core in ((mine_ref, place_ref[1]), (other_ref, 1 - place_ref[1])):
            lines = rows_ref[here, :, :, pl.ds(pl.multiple_of(core * half, half), half)].reshape(tall, half)
            product = jnp.dot(lines, ref[...], preferred_element_type=jnp.float32)
            total = product if total is None else total + product
        for d, out_ref in enumerate(outs):
            out_ref[step * tall : (step + 1) * tall] = total[:, d * width : (d + 1) * width].astype(out_ref.dtype)


def base_parts(place, gathered, mine, other, width_out):
    nz, ny, rows, part = gathered.shape
    near = pl.BlockSpec(memory_space=pltpu.VMEM)
    return pl.pallas_call(
        base_kernel,
        out_shape=[jax.ShapeDtypeStruct((ny * nz * rows, width_out), gathered.dtype)] * ny,
        in_specs=[pl.BlockSpec(memory_space=pltpu.SMEM), near, near, near],
        out_specs=[near] * ny,
        compiler_params=pltpu.CompilerParams(vmem_limit_bytes=14 * mebibyte),
        cost_estimate=pl.CostEstimate(
            flops=2 * ny * nz * rows * part * ny * width_out, bytes_accessed=10 * mebibyte, transcendentals=0
        ),
        name="base_parts",
    )(place, gathered, mine, other)


def lower_kernel(count, parts_ref, ids_ref, out_ref):
    total = jnp.sum(parts_ref[...].astype(jnp.float32), axis=0)
    rank = total.shape[1] // count
    ids = ids_ref[:, :rank]
    low = jnp.zeros((total.shape[0], rank), jnp.float32)
    for s in range(count):
        low += jnp.where(ids == s, total[:, s * rank : (s + 1) * rank], 0.0)
    low = jnp.concatenate([low, ids.astype(jnp.float32)], axis=1).astype(out_ref.dtype)
    for k in range(out_ref.shape[0]):
        out_ref[k] = low


def lower_parts(parts, ids, count):
    pieces, rows, wide = parts.shape
    near = pl.BlockSpec(memory_space=pltpu.VMEM)
    return pl.pallas_call(
        functools.partial(lower_kernel, count),
        out_shape=jax.ShapeDtypeStruct((pieces, rows, 2 * wide // count), parts.dtype),
        in_specs=[near, near],
        out_specs=near,
        compiler_params=pltpu.CompilerParams(vmem_limit_bytes=8 * mebibyte),
        cost_estimate=pl.CostEstimate(flops=0, bytes_accessed=mebibyte, transcendentals=0),
        name="lower_parts",
    )(parts, ids)


def final_kernel(place_ref, low_ref, up_ref, *rest):
    base, out_ref = rest[:-1], rest[-1]
    ny = len(base)
    nz, _, rows, width = base[0].shape
    count, rank, _ = up_ref.shape
    block = nz * rows
    low = low_ref[...].reshape(ny * block, 2 * rank).astype(jnp.float32)
    low, ids = low[:, :rank], low[:, rank:]
    low = jnp.concatenate([low, low], axis=1)
    ids = jnp.concatenate([ids, ids], axis=1)
    lane = lax.broadcasted_iota(jnp.int32, low.shape, 1)
    kept = [
        jnp.where(ids == jnp.where(lane < rank, float(s), float(s + 1)), low, 0.0).astype(jnp.bfloat16)
        for s in range(0, count, 2)
    ]
    up = up_ref[...].reshape(count * rank, width)
    update = jnp.dot(jnp.concatenate(kept, axis=1), up, preferred_element_type=jnp.float32)
    for owner in range(ny):
        total = adapter_scale * update[owner * block : (owner + 1) * block]
        for d, ref in enumerate(base):
            back = (place_ref[2] + d + ny - owner) % ny
            total += ref[:, pl.ds(back, 1)].reshape(block, width).astype(jnp.float32)
        out_ref[owner * block : (owner + 1) * block] = total.astype(out_ref.dtype)


def final_rows(place, low, ups, base, ny, nz):
    tall, width_out = base[0].shape
    count, rank, _ = ups.shape
    near = pl.BlockSpec(memory_space=pltpu.VMEM)
    return pl.pallas_call(
        final_kernel,
        out_shape=jax.ShapeDtypeStruct((tall, width_out), jnp.bfloat16),
        in_specs=[pl.BlockSpec(memory_space=pltpu.SMEM)] + [near] * (2 + len(base)),
        out_specs=near,
        compiler_params=pltpu.CompilerParams(vmem_limit_bytes=16 * mebibyte),
        cost_estimate=pl.CostEstimate(
            flops=2 * tall * count * rank * width_out, bytes_accessed=4 * mebibyte, transcendentals=0
        ),
        name="final_rows",
    )(place, low, ups, *[part.reshape(nz, ny, tall // (ny * nz), width_out) for part in base])


def per_device(nx, nc, ny, nz, tokens, base_weight, down_pool, up_pool, slot_of, requested, row_adapter):
    rows, width = tokens.shape
    width_out = base_weight.shape[1]
    held, rank, _ = down_pool.shape
    count_new = requested.shape[0]
    part = width // ny
    sub = part // (nx * nc)
    nt = ny * nz
    x, core, y, z = [lax.axis_index(a).astype(jnp.int32) for a in ("x", "core", "y", "z")]
    place = jnp.stack([x, core, y, z])

    sent = send_parts(place, tokens, ny)
    pools = cut_parts([up_pool, after(down_pool, sent[1])], ny)
    arrived = [after(sent[0], pools)] + [shift(sent[d], "y", ny, d) for d in range(1, ny)]
    far = jnp.concatenate(arrived)
    gathered = lax.all_gather(far, "z", axis=0, tiled=True).reshape(nz, ny, rows, part)

    weights = base_weight.reshape(ny * nc * nx, sub, width_out)
    piece = [
        lax.dynamic_index_in_dim(weights, (y + d) % ny * (nc * nx) + core * nx + x, 0, keepdims=False)
        for d in range(ny)
    ]
    piece = [shift(after(block, sent[1]), "y", ny, d) if d else block for d, block in enumerate(piece)]

    pools = swap(after(pools, far, *piece), "y").reshape(ny * 2 * held, rank, part)
    piece = jnp.concatenate(piece, axis=1)

    pool_rows = slot_of[requested]
    home, local = pool_rows // held, pool_rows % held
    home_y, home_z = home // nz, home % nz
    slots = home_y * (2 * held) + local

    piece = order_parts(place, [shift(piece, "x", nx, e) if e else piece for e in range(nx)])
    other = shift(piece, "core", nc, 1)

    wanted = (home_z == z).astype(jnp.int32)
    slots = jnp.concatenate([slots, slots + held])
    chosen, ups = local_parts(place, wanted, slots, gathered, pools, width_out)
    ups = lax.psum_scatter(ups, "z", scatter_dimension=0, tiled=True)[0]
    base = base_parts(after(place, chosen), gathered, piece, other, width_out)
    base = [shift(part, "y", ny, ny - d) if d else part for d, part in enumerate(base)]
    ids = jnp.broadcast_to(row_adapter[:, None], (rows, 2 * rank))
    lowered = swap(lower_parts(swap(chosen, ("y", "z")), ids, count_new), ("y", "z"))
    return final_rows(place, lowered, ups, base, ny, nz)


def solution(mesh):
    nx, nc, ny, nz = 4, 2, 4, 8
    fine = Mesh(mesh.devices.reshape(nx, nc, ny, nz), ("x", "core", "y", "z"))
    group, tensor = ("x", "core"), ("y", "z")
    both = group + tensor
    placed = (
        P(both, None),
        P(None, tensor),
        P(both, None, None),
        P(both, None, None),
        P(group),
        P(group),
        P(both),
    )

    def step(*args):
        return per_device(nx, nc, ny, nz, *args)

    return jax.shard_map(step, mesh=fine, in_specs=placed, out_specs=P(group, tensor), check_vma=False)
```

```python
import functools

import jax
import jax.numpy as jnp
from jax import lax
from jax.experimental import pallas as pl
from jax.experimental.pallas import tpu as pltpu
from jax.sharding import Mesh, PartitionSpec as P

adapter_scale = 2.0
mebibyte = 1024 * 1024


def swap(value, axis):
    return lax.all_to_all(value, axis, split_axis=0, concat_axis=0, tiled=True)


def after(value, *earlier):
    return lax.optimization_barrier((value,) + earlier)[0]


def shift(value, axis, size, by):
    return lax.ppermute(value, axis, [(i, (i + by) % size) for i in range(size)])


def send_kernel(place_ref, tokens_ref, *outs):
    part = outs[0].shape[1]
    for d, out_ref in enumerate(outs):
        first = (place_ref[2] + d) % len(outs) * part
        out_ref[...] = tokens_ref[:, pl.ds(pl.multiple_of(first, part), part)]


def send_parts(place, tokens, count):
    rows, width = tokens.shape
    near = pl.BlockSpec(memory_space=pltpu.VMEM)
    return pl.pallas_call(
        send_kernel,
        out_shape=[jax.ShapeDtypeStruct((rows, width // count), tokens.dtype)] * count,
        in_specs=[pl.BlockSpec(memory_space=pltpu.SMEM), near],
        out_specs=[near] * count,
        compiler_params=pltpu.CompilerParams(vmem_limit_bytes=8 * mebibyte),
        cost_estimate=pl.CostEstimate(flops=0, bytes_accessed=mebibyte, transcendentals=0),
        name="send_parts",
    )(place, tokens)


def cut_kernel(*refs):
    count = len(refs) // 2 - 1
    pools, out, held, arrived, left = refs[:count], refs[count], refs[count + 1 : -2], refs[-2], refs[-1]
    slots = pools[0].shape[0]
    part = out.shape[3]

    def pool_of(j):
        return pltpu.make_async_copy(pools[j], held[j], arrived.at[j])

    def piece_of(j, k):
        source = held[j].at[:, :, pl.ds(k * part, part)]
        return pltpu.make_async_copy(source, out.at[k, pl.ds(j * slots, slots)], left.at[j, k])

    for j in range(count):
        pool_of(j).start()
    for j in range(count):
        pool_of(j).wait()
        for k in range(out.shape[0]):
            piece_of(j, k).start()
    for j in range(count):
        for k in range(out.shape[0]):
            piece_of(j, k).wait()


def cut_parts(pools, count):
    held, rank, width = pools[0].shape
    where = pl.BlockSpec(memory_space=pl.ANY)
    return pl.pallas_call(
        cut_kernel,
        out_shape=jax.ShapeDtypeStruct((count, len(pools) * held, rank, width // count), pools[0].dtype),
        in_specs=[where] * len(pools),
        out_specs=where,
        scratch_shapes=[pltpu.VMEM(p.shape, p.dtype) for p in pools]
        + [pltpu.SemaphoreType.DMA((len(pools),)), pltpu.SemaphoreType.DMA((len(pools), count))],
        compiler_params=pltpu.CompilerParams(vmem_limit_bytes=60 * mebibyte),
        cost_estimate=pl.CostEstimate(flops=0, bytes_accessed=8 * mebibyte, transcendentals=0),
        name="cut_parts",
    )(*pools)


def order_kernel(place_ref, *refs):
    out_ref = refs[-1]
    count = len(refs) - 1
    sub = refs[0].shape[0]
    for e in range(count):
        first = (place_ref[0] + count - e) % count * sub
        out_ref[pl.ds(pl.multiple_of(first, sub), sub)] = refs[e][...]


def order_parts(place, pieces):
    sub, wide = pieces[0].shape
    near = pl.BlockSpec(memory_space=pltpu.VMEM)
    return pl.pallas_call(
        order_kernel,
        out_shape=jax.ShapeDtypeStruct((len(pieces) * sub, wide), pieces[0].dtype),
        in_specs=[pl.BlockSpec(memory_space=pltpu.SMEM)] + [near] * len(pieces),
        out_specs=near,
        compiler_params=pltpu.CompilerParams(vmem_limit_bytes=8 * mebibyte),
        cost_estimate=pl.CostEstimate(flops=0, bytes_accessed=4 * mebibyte, transcendentals=0),
        name="order_parts",
    )(place, *pieces)


def local_kernel(
    place_ref, wanted_ref, slot_ref, rows_ref, pool_ref, out_ref, ups_ref, down_ref, up_ref, downed, upped
):
    nz, ny, rows, part = rows_ref.shape
    rank = pool_ref.shape[1]
    count = slot_ref.shape[0] // 2
    width = ups_ref.shape[3]
    steps = 2
    share = nz // steps

    def up_of(s):
        return pltpu.make_async_copy(pool_ref.at[slot_ref[s]], up_ref.at[s], upped.at[s])

    def down_of(s):
        lines = pl.ds(s * rank, rank)
        return pltpu.make_async_copy(pool_ref.at[slot_ref[count + s]], down_ref.at[lines], downed.at[s])

    for s in range(count):
        down_of(s).start()
    for s in range(count):
        up_of(s).start()
    for s in range(count):
        down_of(s).wait()

    lane = lax.broadcasted_iota(jnp.int32, (rows, count * rank), 1) // rank
    wanted = lane < 0
    for s in range(count):
        wanted = wanted | ((lane == s) & (wanted_ref[s] != 0))
    for i in range(steps):
        product = lax.dot_general(
            rows_ref[i * share : (i + 1) * share].reshape(share * ny * rows, part),
            down_ref[...],
            (((1,), (1,)), ((), ())),
            preferred_element_type=jnp.float32,
        )
        for j in range(share):
            for k in range(ny):
                first = (j * ny + k) * rows
                piece = jnp.where(wanted, product[first : first + rows], 0.0)
                out_ref[(place_ref[2] + ny - k) % ny * nz + i * share + j] = piece.astype(out_ref.dtype)
    for s in range(count):
        up_of(s).wait()
        for k in range(nz):
            piece = up_ref[s, :, k * width : (k + 1) * width]
            ups_ref[k, s] = jnp.where(wanted_ref[s] != 0, piece, jnp.zeros_like(piece))


def local_parts(place, wanted, slots, gathered, pools, width_out):
    nz, ny, rows, part = gathered.shape
    _, rank, _ = pools.shape
    count = wanted.shape[0]
    kind = gathered.dtype
    scalars = pl.BlockSpec(memory_space=pltpu.SMEM)
    where = pl.BlockSpec(memory_space=pl.ANY)
    near = pl.BlockSpec(memory_space=pltpu.VMEM)
    return pl.pallas_call(
        local_kernel,
        out_shape=[
            jax.ShapeDtypeStruct((ny * nz, rows, count * rank), kind),
            jax.ShapeDtypeStruct((nz, count, rank, width_out), kind),
        ],
        in_specs=[scalars, scalars, scalars, near, where],
        out_specs=[near, near],
        scratch_shapes=[
            pltpu.VMEM((count * rank, part), kind),
            pltpu.VMEM((count, rank, part), kind),
            pltpu.SemaphoreType.DMA((count,)),
            pltpu.SemaphoreType.DMA((count,)),
        ],
        compiler_params=pltpu.CompilerParams(vmem_limit_bytes=14 * mebibyte),
        cost_estimate=pl.CostEstimate(
            flops=2 * ny * nz * rows * part * count * rank, bytes_accessed=8 * mebibyte, transcendentals=0
        ),
        name="local_parts",
    )(place, wanted, slots, gathered, pools)


def base_kernel(place_ref, rows_ref, mine_ref, other_ref, *outs):
    nz, ny, rows, part = rows_ref.shape
    half = mine_ref.shape[0]
    width = outs[0].shape[1]
    steps = 2
    tall = nz // steps * ny * rows
    for step in range(steps):
        here = pl.ds(step * (nz // steps), nz // steps)
        total = None
        for ref, core in ((mine_ref, place_ref[1]), (other_ref, 1 - place_ref[1])):
            lines = rows_ref[here, :, :, pl.ds(pl.multiple_of(core * half, half), half)].reshape(tall, half)
            product = jnp.dot(lines, ref[...], preferred_element_type=jnp.float32)
            total = product if total is None else total + product
        for d, out_ref in enumerate(outs):
            out_ref[step * tall : (step + 1) * tall] = total[:, d * width : (d + 1) * width].astype(out_ref.dtype)


def base_parts(place, gathered, mine, other, width_out):
    nz, ny, rows, part = gathered.shape
    near = pl.BlockSpec(memory_space=pltpu.VMEM)
    return pl.pallas_call(
        base_kernel,
        out_shape=[jax.ShapeDtypeStruct((ny * nz * rows, width_out), gathered.dtype)] * ny,
        in_specs=[pl.BlockSpec(memory_space=pltpu.SMEM), near, near, near],
        out_specs=[near] * ny,
        compiler_params=pltpu.CompilerParams(vmem_limit_bytes=14 * mebibyte),
        cost_estimate=pl.CostEstimate(
            flops=2 * ny * nz * rows * part * ny * width_out, bytes_accessed=10 * mebibyte, transcendentals=0
        ),
        name="base_parts",
    )(place, gathered, mine, other)


def lower_kernel(count, parts_ref, ids_ref, out_ref):
    total = jnp.sum(parts_ref[...].astype(jnp.float32), axis=0)
    rank = total.shape[1] // count
    ids = ids_ref[:, :rank]
    low = jnp.zeros((total.shape[0], rank), jnp.float32)
    for s in range(count):
        low += jnp.where(ids == s, total[:, s * rank : (s + 1) * rank], 0.0)
    low = jnp.concatenate([low, ids.astype(jnp.float32)], axis=1).astype(out_ref.dtype)
    for k in range(out_ref.shape[0]):
        out_ref[k] = low


def lower_parts(parts, ids, count):
    pieces, rows, wide = parts.shape
    near = pl.BlockSpec(memory_space=pltpu.VMEM)
    return pl.pallas_call(
        functools.partial(lower_kernel, count),
        out_shape=jax.ShapeDtypeStruct((pieces, rows, 2 * wide // count), parts.dtype),
        in_specs=[near, near],
        out_specs=near,
        compiler_params=pltpu.CompilerParams(vmem_limit_bytes=8 * mebibyte),
        cost_estimate=pl.CostEstimate(flops=0, bytes_accessed=mebibyte, transcendentals=0),
        name="lower_parts",
    )(parts, ids)


def final_kernel(place_ref, low_ref, up_ref, *rest):
    base, (out_ref, own_ref, arrived) = rest[:-3], rest[-3:]
    copy = pltpu.make_async_copy(base[0], own_ref, arrived)
    copy.start()
    base = (own_ref,) + base[1:]
    ny = len(base)
    nz, _, rows, width = base[0].shape
    count, rank, _ = up_ref.shape
    block = nz * rows
    low = low_ref[...].reshape(ny * block, 2 * rank).astype(jnp.float32)
    low, ids = low[:, :rank], low[:, rank:]
    low = jnp.concatenate([low, low], axis=1)
    ids = jnp.concatenate([ids, ids], axis=1)
    lane = lax.broadcasted_iota(jnp.int32, low.shape, 1)
    kept = [
        jnp.where(ids == jnp.where(lane < rank, float(s), float(s + 1)), low, 0.0).astype(jnp.bfloat16)
        for s in range(0, count, 2)
    ]
    up = up_ref[...].reshape(count * rank, width)
    update = jnp.dot(jnp.concatenate(kept, axis=1), up, preferred_element_type=jnp.float32)
    copy.wait()
    for owner in range(ny):
        total = adapter_scale * update[owner * block : (owner + 1) * block]
        for d, ref in enumerate(base):
            back = (place_ref[2] + d + ny - owner) % ny
            total += ref[:, pl.ds(back, 1)].reshape(block, width).astype(jnp.float32)
        out_ref[owner * block : (owner + 1) * block] = total.astype(out_ref.dtype)


def final_rows(place, low, ups, base, ny, nz):
    tall, width_out = base[0].shape
    count, rank, _ = ups.shape
    near = pl.BlockSpec(memory_space=pltpu.VMEM)
    return pl.pallas_call(
        final_kernel,
        out_shape=jax.ShapeDtypeStruct((tall, width_out), jnp.bfloat16),
        in_specs=[pl.BlockSpec(memory_space=pltpu.SMEM)] + [near] * 2
        + [pl.BlockSpec(memory_space=pl.ANY)]
        + [near] * (len(base) - 1),
        out_specs=near,
        scratch_shapes=[
            pltpu.VMEM((nz, ny, tall // (ny * nz), width_out), base[0].dtype),
            pltpu.SemaphoreType.DMA,
        ],
        compiler_params=pltpu.CompilerParams(vmem_limit_bytes=16 * mebibyte),
        cost_estimate=pl.CostEstimate(
            flops=2 * tall * count * rank * width_out, bytes_accessed=4 * mebibyte, transcendentals=0
        ),
        name="final_rows",
    )(place, low, ups, *[part.reshape(nz, ny, tall // (ny * nz), width_out) for part in base])


def per_device(nx, nc, ny, nz, tokens, base_weight, down_pool, up_pool, slot_of, requested, row_adapter):
    rows, width = tokens.shape
    width_out = base_weight.shape[1]
    held, rank, _ = down_pool.shape
    count_new = requested.shape[0]
    part = width // ny
    sub = part // (nx * nc)
    nt = ny * nz
    x, core, y, z = [lax.axis_index(a).astype(jnp.int32) for a in ("x", "core", "y", "z")]
    place = jnp.stack([x, core, y, z])

    sent = send_parts(place, tokens, ny)
    pools = cut_parts([up_pool, after(down_pool, sent[1])], ny)
    arrived = [after(sent[0], pools)] + [shift(sent[d], "y", ny, d) for d in range(1, ny)]
    far = jnp.concatenate(arrived)
    gathered = lax.all_gather(far, "z", axis=0, tiled=True).reshape(nz, ny, rows, part)

    weights = base_weight.reshape(ny * nc * nx, sub, width_out)
    piece = [
        lax.dynamic_index_in_dim(weights, (y + d) % ny * (nc * nx) + core * nx + x, 0, keepdims=False)
        for d in range(ny)
    ]
    piece = [shift(after(block, sent[1]), "y", ny, d) if d else block for d, block in enumerate(piece)]

    pools = swap(after(pools, far, *piece), "y").reshape(ny * 2 * held, rank, part)
    piece = jnp.concatenate(piece, axis=1)

    pool_rows = slot_of[requested]
    home, local = pool_rows // held, pool_rows % held
    home_y, home_z = home // nz, home % nz
    slots = home_y * (2 * held) + local

    piece = order_parts(place, [shift(piece, "x", nx, e) if e else piece for e in range(nx)])
    other = shift(piece, "core", nc, 1)

    wanted = (home_z == z).astype(jnp.int32)
    slots = jnp.concatenate([slots, slots + held])
    chosen, ups = local_parts(place, wanted, slots, gathered, pools, width_out)
    ups = lax.psum_scatter(ups, "z", scatter_dimension=0, tiled=True)[0]
    base = base_parts(after(place, chosen), gathered, piece, other, width_out)
    base = [shift(part, "y", ny, ny - d) if d else part for d, part in enumerate(base)]
    ids = jnp.broadcast_to(row_adapter[:, None], (rows, 2 * rank))
    lowered = swap(lower_parts(swap(chosen, ("y", "z")), ids, count_new), ("y", "z"))
    return final_rows(place, lowered, ups, base, ny, nz)


def solution(mesh):
    nx, nc, ny, nz = 4, 2, 4, 8
    fine = Mesh(mesh.devices.reshape(nx, nc, ny, nz), ("x", "core", "y", "z"))
    group, tensor = ("x", "core"), ("y", "z")
    both = group + tensor
    placed = (
        P(both, None),
        P(None, tensor),
        P(both, None, None),
        P(both, None, None),
        P(group),
        P(group),
        P(both),
    )

    def step(*args):
        return per_device(nx, nc, ny, nz, *args)

    return jax.shard_map(step, mesh=fine, in_specs=placed, out_specs=P(group, tensor), check_vma=False)
```

```python
import functools

import jax
import jax.numpy as jnp
from jax import lax
from jax.experimental import pallas as pl
from jax.experimental.pallas import tpu as pltpu
from jax.sharding import Mesh, PartitionSpec as P

adapter_scale = 2.0
mebibyte = 1024 * 1024


def swap(value, axis):
    return lax.all_to_all(value, axis, split_axis=0, concat_axis=0, tiled=True)


def after(value, *earlier):
    return lax.optimization_barrier((value,) + earlier)[0]


def shift(value, axis, size, by):
    return lax.ppermute(value, axis, [(i, (i + by) % size) for i in range(size)])


def send_kernel(place_ref, tokens_ref, *outs):
    part = outs[0].shape[1]
    for d, out_ref in enumerate(outs):
        first = (place_ref[2] + d) % len(outs) * part
        out_ref[...] = tokens_ref[:, pl.ds(pl.multiple_of(first, part), part)]


def send_parts(place, tokens, count):
    rows, width = tokens.shape
    near = pl.BlockSpec(memory_space=pltpu.VMEM)
    return pl.pallas_call(
        send_kernel,
        out_shape=[jax.ShapeDtypeStruct((rows, width // count), tokens.dtype)] * count,
        in_specs=[pl.BlockSpec(memory_space=pltpu.SMEM), near],
        out_specs=[near] * count,
        compiler_params=pltpu.CompilerParams(vmem_limit_bytes=8 * mebibyte),
        cost_estimate=pl.CostEstimate(flops=0, bytes_accessed=mebibyte, transcendentals=0),
        name="send_parts",
    )(place, tokens)


def cut_kernel(*refs):
    count = len(refs) // 2 - 1
    pools, out, held, arrived, left = refs[:count], refs[count], refs[count + 1 : -2], refs[-2], refs[-1]
    slots = pools[0].shape[0]
    part = out.shape[3]

    def pool_of(j):
        return pltpu.make_async_copy(pools[j], held[j], arrived.at[j])

    def piece_of(j, k):
        source = held[j].at[:, :, pl.ds(k * part, part)]
        return pltpu.make_async_copy(source, out.at[k, pl.ds(j * slots, slots)], left.at[j, k])

    for j in range(count):
        pool_of(j).start()
    for j in range(count):
        pool_of(j).wait()
        for k in range(out.shape[0]):
            piece_of(j, k).start()
    for j in range(count):
        for k in range(out.shape[0]):
            piece_of(j, k).wait()


def cut_parts(pools, count):
    held, rank, width = pools[0].shape
    where = pl.BlockSpec(memory_space=pl.ANY)
    return pl.pallas_call(
        cut_kernel,
        out_shape=jax.ShapeDtypeStruct((count, len(pools) * held, rank, width // count), pools[0].dtype),
        in_specs=[where] * len(pools),
        out_specs=where,
        scratch_shapes=[pltpu.VMEM(p.shape, p.dtype) for p in pools]
        + [pltpu.SemaphoreType.DMA((len(pools),)), pltpu.SemaphoreType.DMA((len(pools), count))],
        compiler_params=pltpu.CompilerParams(vmem_limit_bytes=60 * mebibyte),
        cost_estimate=pl.CostEstimate(flops=0, bytes_accessed=8 * mebibyte, transcendentals=0),
        name="cut_parts",
    )(*pools)


def order_kernel(place_ref, *refs):
    out_ref = refs[-1]
    count = len(refs) - 1
    sub = refs[0].shape[0]
    for e in range(count):
        first = (place_ref[0] + count - e) % count * sub
        out_ref[pl.ds(pl.multiple_of(first, sub), sub)] = refs[e][...]


def order_parts(place, pieces):
    sub, wide = pieces[0].shape
    near = pl.BlockSpec(memory_space=pltpu.VMEM)
    return pl.pallas_call(
        order_kernel,
        out_shape=jax.ShapeDtypeStruct((len(pieces) * sub, wide), pieces[0].dtype),
        in_specs=[pl.BlockSpec(memory_space=pltpu.SMEM)] + [near] * len(pieces),
        out_specs=near,
        compiler_params=pltpu.CompilerParams(vmem_limit_bytes=8 * mebibyte),
        cost_estimate=pl.CostEstimate(flops=0, bytes_accessed=4 * mebibyte, transcendentals=0),
        name="order_parts",
    )(place, *pieces)


def local_kernel(
    place_ref, wanted_ref, slot_ref, rows_ref, pool_ref, out_ref, ups_ref, down_ref, up_ref, downed, upped
):
    nz, ny, rows, part = rows_ref.shape
    rank = pool_ref.shape[1]
    count = slot_ref.shape[0] // 2
    width = ups_ref.shape[3]
    steps = 2
    share = nz // steps

    def up_of(s):
        return pltpu.make_async_copy(pool_ref.at[slot_ref[s]], up_ref.at[s], upped.at[s])

    def down_of(s):
        lines = pl.ds(s * rank, rank)
        return pltpu.make_async_copy(pool_ref.at[slot_ref[count + s]], down_ref.at[lines], downed.at[s])

    for s in range(count):
        down_of(s).start()
    for s in range(count):
        up_of(s).start()
    for s in range(count):
        down_of(s).wait()

    lane = lax.broadcasted_iota(jnp.int32, (rows, count * rank), 1) // rank
    wanted = lane < 0
    for s in range(count):
        wanted = wanted | ((lane == s) & (wanted_ref[s] != 0))
    for i in range(steps):
        product = lax.dot_general(
            rows_ref[i * share : (i + 1) * share].reshape(share * ny * rows, part),
            down_ref[...],
            (((1,), (1,)), ((), ())),
            preferred_element_type=jnp.float32,
        )
        for j in range(share):
            for k in range(ny):
                first = (j * ny + k) * rows
                piece = jnp.where(wanted, product[first : first + rows], 0.0)
                out_ref[(place_ref[2] + ny - k) % ny * nz + i * share + j] = piece.astype(out_ref.dtype)
    for s in range(count):
        up_of(s).wait()
        for k in range(nz):
            piece = up_ref[s, :, k * width : (k + 1) * width]
            ups_ref[k, s] = jnp.where(wanted_ref[s] != 0, piece, jnp.zeros_like(piece))


def local_parts(place, wanted, slots, gathered, pools, width_out):
    nz, ny, rows, part = gathered.shape
    _, rank, _ = pools.shape
    count = wanted.shape[0]
    kind = gathered.dtype
    scalars = pl.BlockSpec(memory_space=pltpu.SMEM)
    where = pl.BlockSpec(memory_space=pl.ANY)
    near = pl.BlockSpec(memory_space=pltpu.VMEM)
    return pl.pallas_call(
        local_kernel,
        out_shape=[
            jax.ShapeDtypeStruct((ny * nz, rows, count * rank), kind),
            jax.ShapeDtypeStruct((nz, count, rank, width_out), kind),
        ],
        in_specs=[scalars, scalars, scalars, near, where],
        out_specs=[near, near],
        scratch_shapes=[
            pltpu.VMEM((count * rank, part), kind),
            pltpu.VMEM((count, rank, part), kind),
            pltpu.SemaphoreType.DMA((count,)),
            pltpu.SemaphoreType.DMA((count,)),
        ],
        compiler_params=pltpu.CompilerParams(vmem_limit_bytes=14 * mebibyte),
        cost_estimate=pl.CostEstimate(
            flops=2 * ny * nz * rows * part * count * rank, bytes_accessed=8 * mebibyte, transcendentals=0
        ),
        name="local_parts",
    )(place, wanted, slots, gathered, pools)


def base_kernel(place_ref, rows_ref, mine_ref, other_ref, *outs):
    nz, ny, rows, part = rows_ref.shape
    half = mine_ref.shape[0]
    width = outs[0].shape[1]
    steps = 2
    tall = nz // steps * ny * rows
    for step in range(steps):
        here = pl.ds(step * (nz // steps), nz // steps)
        total = None
        for ref, core in ((mine_ref, place_ref[1]), (other_ref, 1 - place_ref[1])):
            lines = rows_ref[here, :, :, pl.ds(pl.multiple_of(core * half, half), half)].reshape(tall, half)
            product = jnp.dot(lines, ref[...], preferred_element_type=jnp.float32)
            total = product if total is None else total + product
        for d, out_ref in enumerate(outs):
            out_ref[step * tall : (step + 1) * tall] = total[:, d * width : (d + 1) * width].astype(out_ref.dtype)


def base_parts(place, gathered, mine, other, width_out):
    nz, ny, rows, part = gathered.shape
    near = pl.BlockSpec(memory_space=pltpu.VMEM)
    return pl.pallas_call(
        base_kernel,
        out_shape=[jax.ShapeDtypeStruct((ny * nz * rows, width_out), gathered.dtype)] * ny,
        in_specs=[pl.BlockSpec(memory_space=pltpu.SMEM), near, near, near],
        out_specs=[near] * ny,
        compiler_params=pltpu.CompilerParams(vmem_limit_bytes=14 * mebibyte),
        cost_estimate=pl.CostEstimate(
            flops=2 * ny * nz * rows * part * ny * width_out, bytes_accessed=10 * mebibyte, transcendentals=0
        ),
        name="base_parts",
    )(place, gathered, mine, other)


def lower_kernel(count, parts_ref, ids_ref, out_ref):
    total = jnp.sum(parts_ref[...].astype(jnp.float32), axis=0)
    rank = total.shape[1] // count
    ids = ids_ref[:, :rank]
    low = jnp.zeros((total.shape[0], rank), jnp.float32)
    for s in range(count):
        low += jnp.where(ids == s, total[:, s * rank : (s + 1) * rank], 0.0)
    low = jnp.concatenate([low, ids.astype(jnp.float32)], axis=1).astype(out_ref.dtype)
    for k in range(out_ref.shape[0]):
        out_ref[k] = low


def lower_parts(parts, ids, count):
    pieces, rows, wide = parts.shape
    near = pl.BlockSpec(memory_space=pltpu.VMEM)
    return pl.pallas_call(
        functools.partial(lower_kernel, count),
        out_shape=jax.ShapeDtypeStruct((pieces, rows, 2 * wide // count), parts.dtype),
        in_specs=[near, near],
        out_specs=near,
        compiler_params=pltpu.CompilerParams(vmem_limit_bytes=8 * mebibyte),
        cost_estimate=pl.CostEstimate(flops=0, bytes_accessed=mebibyte, transcendentals=0),
        name="lower_parts",
    )(parts, ids)


def final_kernel(place_ref, low_ref, up_ref, *rest):
    base, out_ref = rest[:-1], rest[-1]
    ny = len(base)
    nz, _, rows, width = base[0].shape
    count, rank, _ = up_ref.shape
    block = nz * rows
    low = low_ref[...].reshape(ny * block, 2 * rank).astype(jnp.float32)
    low, ids = low[:, :rank], low[:, rank:]
    low = jnp.concatenate([low, low], axis=1)
    ids = jnp.concatenate([ids, ids], axis=1)
    lane = lax.broadcasted_iota(jnp.int32, low.shape, 1)
    kept = [
        jnp.where(ids == jnp.where(lane < rank, float(s), float(s + 1)), low, 0.0).astype(jnp.bfloat16)
        for s in range(0, count, 2)
    ]
    up = up_ref[...].reshape(count * rank, width)
    update = jnp.dot(jnp.concatenate(kept, axis=1), up, preferred_element_type=jnp.float32)
    for owner in range(ny):
        total = adapter_scale * update[owner * block : (owner + 1) * block]
        for d, ref in enumerate(base):
            back = (place_ref[2] + d + ny - owner) % ny
            total += ref[:, pl.ds(back, 1)].reshape(block, width).astype(jnp.float32)
        out_ref[owner * block : (owner + 1) * block] = total.astype(out_ref.dtype)


def final_rows(place, low, ups, base, ny, nz):
    tall, width_out = base[0].shape
    count, rank, _ = ups.shape
    near = pl.BlockSpec(memory_space=pltpu.VMEM)
    return pl.pallas_call(
        final_kernel,
        out_shape=jax.ShapeDtypeStruct((tall, width_out), jnp.bfloat16),
        in_specs=[pl.BlockSpec(memory_space=pltpu.SMEM)] + [near] * (2 + len(base)),
        out_specs=near,
        compiler_params=pltpu.CompilerParams(vmem_limit_bytes=16 * mebibyte),
        cost_estimate=pl.CostEstimate(
            flops=2 * tall * count * rank * width_out, bytes_accessed=4 * mebibyte, transcendentals=0
        ),
        name="final_rows",
    )(place, low, ups, *[part.reshape(nz, ny, tall // (ny * nz), width_out) for part in base])


def per_device(nx, nc, ny, nz, tokens, base_weight, down_pool, up_pool, slot_of, requested, row_adapter):
    rows, width = tokens.shape
    width_out = base_weight.shape[1]
    held, rank, _ = down_pool.shape
    count_new = requested.shape[0]
    part = width // ny
    sub = part // (nx * nc)
    nt = ny * nz
    x, core, y, z = [lax.axis_index(a).astype(jnp.int32) for a in ("x", "core", "y", "z")]
    place = jnp.stack([x, core, y, z])

    sent = send_parts(place, tokens, ny)
    pools = cut_parts([up_pool, after(down_pool, sent[1])], ny)
    arrived = [after(sent[0], pools)] + [shift(sent[d], "y", ny, d) for d in range(1, ny)]
    far = jnp.concatenate(arrived)
    gathered = lax.all_gather(far, "z", axis=0, tiled=True).reshape(nz, ny, rows, part)

    weights = base_weight.reshape(ny * nc * nx, sub, width_out)
    piece = [
        lax.dynamic_index_in_dim(weights, (y + d) % ny * (nc * nx) + core * nx + x, 0, keepdims=False)
        for d in range(ny)
    ]
    piece = [shift(after(block, sent[1]), "y", ny, d) if d else block for d, block in enumerate(piece)]

    pools = swap(after(pools, far, piece[1]), "y").reshape(ny * 2 * held, rank, part)
    piece = jnp.concatenate(piece, axis=1)

    pool_rows = slot_of[requested]
    home, local = pool_rows // held, pool_rows % held
    home_y, home_z = home // nz, home % nz
    slots = home_y * (2 * held) + local

    piece = order_parts(place, [shift(piece, "x", nx, e) if e else piece for e in range(nx)])
    other = shift(piece, "core", nc, 1)

    wanted = (home_z == z).astype(jnp.int32)
    slots = jnp.concatenate([slots, slots + held])
    chosen, ups = local_parts(place, wanted, slots, gathered, pools, width_out)
    ups = lax.psum_scatter(ups, "z", scatter_dimension=0, tiled=True)[0]
    base = base_parts(after(place, chosen), gathered, piece, other, width_out)
    base = [shift(part, "y", ny, ny - d) if d else part for d, part in enumerate(base)]
    ids = jnp.broadcast_to(row_adapter[:, None], (rows, 2 * rank))
    lowered = swap(lower_parts(swap(chosen, ("y", "z")), ids, count_new), ("y", "z"))
    return final_rows(place, lowered, ups, base, ny, nz)


def solution(mesh):
    nx, nc, ny, nz = 4, 2, 4, 8
    fine = Mesh(mesh.devices.reshape(nx, nc, ny, nz), ("x", "core", "y", "z"))
    group, tensor = ("x", "core"), ("y", "z")
    both = group + tensor
    placed = (
        P(both, None),
        P(None, tensor),
        P(both, None, None),
        P(both, None, None),
        P(group),
        P(group),
        P(both),
    )

    def step(*args):
        return per_device(nx, nc, ny, nz, *args)

    return jax.shard_map(step, mesh=fine, in_specs=placed, out_specs=P(group, tensor), check_vma=False)
```
